32 devices in a mesh: slab: 32 (over z, y, x, core), batch: 1.
Axes of the slice: x: 2, y: 2, z: 4, core: 2. Of those that a mesh axis runs over, the one named last changes fastest.
Arguments:
- field: bfloat16 [1, 128, 64, 128, 128], P('batch', 'slab'), may hold values from -6 to 6
- cotangent: bfloat16 [1, 128, 64, 128, 128], P('batch', 'slab'), may hold values from -6 to 6
- spectral_weight: bfloat16 [2, 64, 64, 16384], P(None, None, None, 'slab'), may hold values from -6 to 6
- w_in: bfloat16 [64, 256], replicated, may hold values from -0.75 to 0.75
- w_out: bfloat16 [256, 64], replicated, may hold values from -0.375 to 0.375
Outputs:
- field_grad: bfloat16 [1, 128, 64, 128, 128], P('batch', 'slab')
- weight_grad: bfloat16 [2, 64, 64, 16384], P('batch', None, None, 'slab')
- in_grad: float32 [64, 256], replicated
- out_grad: float32 [256, 64], replicated
The draws below stay inside these ranges and needn't reach their ends.
All inputs are finite; a program needn't handle non-finite values.
Results may differ from the reference program's by a relative error of at most 0.025.
Values may be sent and summed in bfloat16 or wider, within the bound.
A program may use at most 192 MiB of HBM per device.

```python
import math
import jax
import jax.numpy as jnp
from jax import lax

NX = 128
NY = 128
NZ = 128
C = 64
H = 256
KX = 32
KY = 32
KZ = 16
SAMPLES = 1
MODES = 16384


def levels(own_key, dims, split, low, largest):
    loudness = 1.0
    for dim, shards_of in split:
        draws = jax.random.uniform(jax.random.fold_in(jax.random.fold_in(own_key, 6), dim), (shards_of,), jnp.float32, low / len(split), largest / len(split))
        loudness = loudness * jnp.repeat(jnp.exp(draws), dims[dim] // shards_of).reshape((-1,) + (1,) * (len(dims) - 1 - dim))
    return loudness


def centred(rng, shape, width, most, pieces=(), kind=jnp.bfloat16):
    loudness = levels(rng, shape, pieces, -0.22, 0.18) if pieces else 1.0
    values = jax.random.normal(rng, shape, jnp.float32) * width * loudness
    return jnp.minimum(jnp.maximum(values, -most), most).astype(kind)


def setup_inputs(seed: int = 0) -> dict:
    keys = jax.random.split(jax.random.key(seed), 6)
    field = centred(keys[0], (SAMPLES, NZ, C, NX, NY), 1.0, 6.0, ((1, 32),))
    cotangent = centred(keys[1], (SAMPLES, NZ, C, NX, NY), 1.0, 6.0, ((1, 32),))
    spectral_weight = centred(keys[2], (2, C, C, MODES), 1.0, 6.0, ((3, 32),))
    w_in = centred(keys[3], (C, H), C ** -0.5, 0.75)
    w_out = centred(keys[4], (H, C), H ** -0.5, 0.375)
    return {"field": field, "cotangent": cotangent, "spectral_weight": spectral_weight, "w_in": w_in, "w_out": w_out}


PRECISE = lax.Precision.HIGHEST

def contract(pattern, first_op, second_op):
    return jnp.einsum(pattern, first_op, second_op, precision=PRECISE)

def product_of(pattern, first_op, second_op):
    return jnp.einsum(pattern, first_op.astype(jnp.float32), second_op.astype(jnp.float32), precision=PRECISE)

def tables(length, kept_modes):
    position = jnp.arange(length, dtype=jnp.int32)[:, None]
    frequency = jnp.arange(kept_modes, dtype=jnp.int32)[None, :]
    phases = (position * frequency % length).astype(jnp.float32)
    angles = phases * (2.0 * math.pi / length)
    return (jnp.cos(angles), jnp.sin(angles))

def forward_xy(field_part):
    depth_len, channels, x_len = (field_part.shape[0], field_part.shape[1], field_part.shape[2])
    cos_y, sin_y = tables(field_part.shape[3], KY)
    table_y = jnp.concatenate([cos_y, -sin_y], axis=1).astype(jnp.bfloat16)
    halfway = product_of('zcxy,yk->zckx', field_part, table_y).astype(jnp.bfloat16)
    stacked = halfway.reshape(depth_len, channels, 2, KY, x_len)
    cos_x, sin_x = tables(x_len, KX)
    table_x = jnp.stack([cos_x, sin_x]).astype(jnp.bfloat16)
    parts = product_of('zcpkx,qxj->pqzcjk', stacked, table_x)
    real_xy = parts[0, 0] + parts[1, 1]
    imag_xy = parts[1, 0] - parts[0, 1]
    return jnp.stack([real_xy.reshape(depth_len, channels, -1), imag_xy.reshape(depth_len, channels, -1)])

def forward_z(spectra):
    cos_z, sin_z = tables(spectra.shape[1], KZ)
    real_in, imag_in = (spectra[0], spectra[1])
    real_out = contract('zcm,zk->cmk', real_in, cos_z) + contract('zcm,zk->cmk', imag_in, sin_z)
    imag_out = contract('zcm,zk->cmk', imag_in, cos_z) - contract('zcm,zk->cmk', real_in, sin_z)
    channels = real_in.shape[1]
    return jnp.stack([real_out.reshape(channels, -1), imag_out.reshape(channels, -1)])

def inverse_z(spectrum, depth_len):
    cos_z, sin_z = tables(depth_len, KZ)
    channels = spectrum.shape[1]
    real_in = spectrum[0].reshape(channels, -1, KZ)
    imag_in = spectrum[1].reshape(channels, -1, KZ)
    real_out = contract('cmk,zk->zcm', real_in, cos_z) - contract('cmk,zk->zcm', imag_in, sin_z)
    imag_out = contract('cmk,zk->zcm', real_in, sin_z) + contract('cmk,zk->zcm', imag_in, cos_z)
    return jnp.stack([real_out, imag_out]).astype(jnp.bfloat16)

def inverse_xy(spectra):
    depth_len, channels = (spectra.shape[1], spectra.shape[2])
    stacked = spectra.reshape(2, depth_len, channels, KX, KY)
    cos_x, sin_x = tables(NX, KX)
    table_x = jnp.stack([cos_x, sin_x]).astype(jnp.bfloat16)
    parts = product_of('pzcjk,qxj->pqzckx', stacked, table_x)
    real_x = parts[0, 0] - parts[1, 1]
    imag_x = parts[0, 1] + parts[1, 0]
    rows = jnp.stack([real_x, imag_x]).astype(jnp.bfloat16)
    cos_y, sin_y = tables(NY, KY)
    table_y = jnp.stack([cos_y, -sin_y]).astype(jnp.bfloat16)
    return product_of('pzckx,pyk->zcxy', rows, table_y)

def mode_product(spectrum, weight):
    real_part = product_of('cm,com->om', spectrum[0], weight[0]) - product_of('cm,com->om', spectrum[1], weight[1])
    imag_part = product_of('cm,com->om', spectrum[0], weight[1]) + product_of('cm,com->om', spectrum[1], weight[0])
    return jnp.stack([real_part, imag_part])

def adjoint_product(weight, grad_modes):
    real_part = product_of('com,om->cm', weight[0], grad_modes[0]) + product_of('com,om->cm', weight[1], grad_modes[1])
    imag_part = product_of('com,om->cm', weight[0], grad_modes[1]) - product_of('com,om->cm', weight[1], grad_modes[0])
    return jnp.stack([real_part, imag_part])

def weight_term(spectrum, grad_modes):
    real_part = product_of('cm,om->com', spectrum[0], grad_modes[0]) + product_of('cm,om->com', spectrum[1], grad_modes[1])
    imag_part = product_of('cm,om->com', spectrum[0], grad_modes[1]) - product_of('cm,om->com', spectrum[1], grad_modes[0])
    return jnp.stack([real_part, imag_part])

def inner_last(first_op, second_op):
    return lax.dot_general(first_op, second_op, (((1,), (1,)), ((), ())), preferred_element_type=jnp.float32)

def plane_step(w_in, w_out, plane, spatial, upstream):
    channels = plane.shape[0]
    flat_in = plane.reshape(channels, -1)
    flat_sp = spatial.reshape(channels, -1)
    flat_up = upstream.reshape(channels, -1)
    mixed_field = (flat_in.astype(jnp.float32) + flat_sp).astype(jnp.bfloat16)
    pre_act = lax.dot_general(w_in, mixed_field, (((0,), (0,)), ((), ())), preferred_element_type=jnp.float32)
    active = jax.nn.gelu(pre_act).astype(jnp.bfloat16)
    back_act = jnp.dot(w_out, flat_up, preferred_element_type=jnp.float32)
    pre_grad = jax.vjp(jax.nn.gelu, pre_act)[1](back_act)[0].astype(jnp.bfloat16)
    grad_field = flat_up.astype(jnp.float32) + jnp.dot(w_in, pre_grad, preferred_element_type=jnp.float32)
    term_in = inner_last(mixed_field, pre_grad)
    term_out = inner_last(active, flat_up)
    return (grad_field.reshape(plane.shape), term_in, term_out)

def mlp_planes(field_part, spatial, upstream, w_in, w_out):
    channels, hidden = (w_in.shape[0], w_in.shape[1])

    def advance(running, planes):
        grad_plane, term_in, term_out = plane_step(w_in, w_out, planes[0], planes[1], planes[2])
        return ((running[0] + term_in, running[1] + term_out), grad_plane)
    initial = (jnp.zeros((channels, hidden), jnp.float32), jnp.zeros((hidden, channels), jnp.float32))
    totals, grad_field = lax.scan(advance, initial, (field_part, spatial, upstream))
    return (grad_field, totals[0], totals[1])

def reference(field, cotangent, spectral_weight, w_in, w_out):
    cells = NX * NY * NZ
    in_total = jnp.zeros((C, H), jnp.float32)
    out_total = jnp.zeros((H, C), jnp.float32)
    weight_total = jnp.zeros((2, C, C, MODES), jnp.float32)
    grads = []
    for sample_idx in range(SAMPLES):
        sample = field[sample_idx]
        upstream = cotangent[sample_idx]
        spectrum = forward_z(forward_xy(sample)).astype(jnp.bfloat16)
        mixed_modes = mode_product(spectrum, spectral_weight)
        spatial = inverse_xy(inverse_z(mixed_modes, NZ)) / cells
        grad_field, term_in, term_out = mlp_planes(sample, spatial, upstream, w_in, w_out)
        in_total = in_total + term_in
        out_total = out_total + term_out
        grad_modes = (forward_z(forward_xy(grad_field.astype(jnp.bfloat16))) / cells).astype(jnp.bfloat16)
        sample_term = lax.optimization_barrier(weight_term(spectrum, grad_modes).astype(jnp.bfloat16))
        weight_total = weight_total + sample_term.astype(jnp.float32)
        back_modes = adjoint_product(spectral_weight, grad_modes)
        adjoint = inverse_xy(inverse_z(back_modes, NZ))
        grads.append((grad_field + adjoint).astype(jnp.bfloat16))
    norm_scale = 1.0 / math.sqrt(SAMPLES * NZ * NX * NY)
    return (jnp.stack(grads), weight_total.astype(jnp.bfloat16), in_total * norm_scale, out_total * norm_scale)
```

```python
import math

import jax
import jax.numpy as jnp
from jax import lax
from jax.experimental import pallas as pl
from jax.experimental.pallas import tpu as pltpu
from jax.sharding import PartitionSpec as P

NX = 128
NY = 128
NZ = 128
KX = 32
KY = 32
KZ = 16


PRECISE = lax.Precision.HIGHEST


def contract(pattern, first_op, second_op):
    return jnp.einsum(pattern, first_op, second_op, precision=PRECISE)


def product_of(pattern, first_op, second_op):
    return jnp.einsum(pattern, first_op, second_op, preferred_element_type=jnp.float32)


def tables(length, kept_modes):
    position = jnp.arange(length, dtype=jnp.int32)[:, None]
    frequency = jnp.arange(kept_modes, dtype=jnp.int32)[None, :]
    phases = (position * frequency % length).astype(jnp.float32)
    angles = phases * (2.0 * math.pi / length)
    return (jnp.cos(angles), jnp.sin(angles))


def forward_xy(field_part):
    depth_len, channels, x_len = (field_part.shape[0], field_part.shape[1], field_part.shape[2])
    cos_y, sin_y = tables(field_part.shape[3], KY)
    table_y = jnp.concatenate([cos_y, -sin_y], axis=1).astype(jnp.bfloat16)
    halfway = product_of("zcxy,yk->zckx", field_part, table_y).astype(jnp.bfloat16)
    stacked = halfway.reshape(depth_len, channels, 2, KY, x_len)
    cos_x, sin_x = tables(x_len, KX)
    table_x = jnp.stack([cos_x, sin_x]).astype(jnp.bfloat16)
    parts = product_of("zcpkx,qxj->pqzcjk", stacked, table_x)
    real_xy = parts[0, 0] + parts[1, 1]
    imag_xy = parts[1, 0] - parts[0, 1]
    return jnp.stack(
        [real_xy.reshape(depth_len, channels, -1), imag_xy.reshape(depth_len, channels, -1)]
    )


def forward_z(spectra):
    cos_z, sin_z = tables(spectra.shape[1], KZ)
    real_in, imag_in = (spectra[0], spectra[1])
    real_out = contract("zcm,zk->cmk", real_in, cos_z) + contract("zcm,zk->cmk", imag_in, sin_z)
    imag_out = contract("zcm,zk->cmk", imag_in, cos_z) - contract("zcm,zk->cmk", real_in, sin_z)
    channels = real_in.shape[1]
    return jnp.stack([real_out.reshape(channels, -1), imag_out.reshape(channels, -1)])


def inverse_z(spectrum, depth_len):
    cos_z, sin_z = tables(depth_len, KZ)
    channels = spectrum.shape[1]
    real_in = spectrum[0].reshape(channels, -1, KZ)
    imag_in = spectrum[1].reshape(channels, -1, KZ)
    real_out = contract("cmk,zk->zcm", real_in, cos_z) - contract("cmk,zk->zcm", imag_in, sin_z)
    imag_out = contract("cmk,zk->zcm", real_in, sin_z) + contract("cmk,zk->zcm", imag_in, cos_z)
    return jnp.stack([real_out, imag_out]).astype(jnp.bfloat16)


def inverse_xy(spectra):
    depth_len, channels = (spectra.shape[1], spectra.shape[2])
    stacked = spectra.reshape(2, depth_len, channels, KX, KY)
    cos_x, sin_x = tables(NX, KX)
    table_x = jnp.stack([cos_x, sin_x]).astype(jnp.bfloat16)
    parts = product_of("pzcjk,qxj->pqzckx", stacked, table_x)
    real_x = parts[0, 0] - parts[1, 1]
    imag_x = parts[0, 1] + parts[1, 0]
    rows = jnp.stack([real_x, imag_x]).astype(jnp.bfloat16)
    cos_y, sin_y = tables(NY, KY)
    table_y = jnp.stack([cos_y, -sin_y]).astype(jnp.bfloat16)
    return product_of("pzckx,pyk->zcxy", rows, table_y)


def mode_product(spectrum, weight):
    real_part = product_of("cm,com->om", spectrum[0], weight[0]) - product_of(
        "cm,com->om", spectrum[1], weight[1]
    )
    imag_part = product_of("cm,com->om", spectrum[0], weight[1]) + product_of(
        "cm,com->om", spectrum[1], weight[0]
    )
    return jnp.stack([real_part, imag_part])


def adjoint_product(weight, grad_modes):
    real_part = product_of("com,om->cm", weight[0], grad_modes[0]) + product_of(
        "com,om->cm", weight[1], grad_modes[1]
    )
    imag_part = product_of("com,om->cm", weight[0], grad_modes[1]) - product_of(
        "com,om->cm", weight[1], grad_modes[0]
    )
    return jnp.stack([real_part, imag_part])


def weight_term(spectrum, grad_modes):
    real_part = product_of("cm,om->com", spectrum[0], grad_modes[0]) + product_of(
        "cm,om->com", spectrum[1], grad_modes[1]
    )
    imag_part = product_of("cm,om->com", spectrum[0], grad_modes[1]) - product_of(
        "cm,om->com", spectrum[1], grad_modes[0]
    )
    return jnp.stack([real_part, imag_part])


def inner_last(first_op, second_op):
    return lax.dot_general(
        first_op, second_op, (((1,), (1,)), ((), ())), preferred_element_type=jnp.float32
    )


GELU_A = math.sqrt(2.0 / math.pi)
GELU_B = GELU_A * 0.044715
ROWS = 16
CHUNK = 512


def mlp_kernel(f_ref, s_ref, u_ref, wt_ref, wo_ref, wi_ref, g_ref, ti_ref, to_ref, m_buf, u_buf, g_buf):
    first = (pl.program_id(0) == 0) & (pl.program_id(1) == 0)

    @pl.when(first)
    def _():
        ti_ref[...] = jnp.zeros_like(ti_ref)
        to_ref[...] = jnp.zeros_like(to_ref)

    channels, cells = m_buf.shape
    mixed = f_ref[0].astype(jnp.float32) + s_ref[0].astype(jnp.float32)
    m_buf[...] = mixed.reshape(channels, cells).astype(jnp.bfloat16)
    u_buf[...] = u_ref[0].astype(jnp.float32).reshape(channels, cells).astype(jnp.bfloat16)

    def step(i, _):
        at = pl.ds(pl.multiple_of(i * CHUNK, CHUNK), CHUNK)
        m = m_buf[:, at]
        u = u_buf[:, at]
        x = jnp.dot(wt_ref[...], m, preferred_element_type=jnp.float32)
        back = jnp.dot(wo_ref[...], u, preferred_element_type=jnp.float32)
        sq = x * x
        t = jnp.tanh(x * (GELU_A + GELU_B * sq))
        half = 0.5 + 0.5 * t
        act = x * half
        slope = half + act * (1.0 - t) * (GELU_A + (3.0 * GELU_B) * sq)
        pre_grad = (slope * back).astype(jnp.bfloat16)
        act = act.astype(jnp.bfloat16)
        g = u.astype(jnp.float32) + jnp.dot(
            wi_ref[...], pre_grad, preferred_element_type=jnp.float32
        )
        g_buf[:, at] = g
        ti_ref[...] += inner_last(m, pre_grad)
        to_ref[...] += inner_last(act, u)
        return 0

    lax.fori_loop(0, cells // CHUNK, step, 0)
    g_ref[0] = g_buf[...].reshape(g_ref.shape[1:]).astype(g_ref.dtype)


def mlp_planes(field_part, spatial, upstream, w_in, w_out):
    depth, channels, x_len, y_len = field_part.shape
    hidden = w_in.shape[1]
    block = pl.BlockSpec((1, channels, ROWS, y_len), lambda z, i: (z, 0, i, 0))
    whole = lambda shape: pl.BlockSpec(shape, lambda z, i: (0, 0))
    cells = ROWS * y_len
    return pl.pallas_call(
        mlp_kernel,
        grid=(depth, x_len // ROWS),
        in_specs=[block, block, block, whole((hidden, channels)), whole((hidden, channels)), whole((channels, hidden))],
        out_specs=[block, whole((channels, hidden)), whole((hidden, channels))],
        out_shape=[
            jax.ShapeDtypeStruct(field_part.shape, jnp.bfloat16),
            jax.ShapeDtypeStruct((channels, hidden), jnp.float32),
            jax.ShapeDtypeStruct((hidden, channels), jnp.float32),
        ],
        scratch_shapes=[
            pltpu.VMEM((channels, cells), jnp.bfloat16),
            pltpu.VMEM((channels, cells), jnp.bfloat16),
            pltpu.VMEM((channels, cells), jnp.float32),
        ],
        compiler_params=pltpu.CompilerParams(vmem_limit_bytes=48 * 1024 * 1024),
    )(field_part, spatial, upstream, w_in.T, w_out, w_in)


def gather_modes(spectra):
    return forward_z(
        lax.all_to_all(
            spectra.astype(jnp.bfloat16), "slab", split_axis=3, concat_axis=1, tiled=True
        ).astype(spectra.dtype)
    )


def return_slabs(profiles):
    return inverse_xy(lax.all_to_all(profiles, "slab", split_axis=1, concat_axis=3, tiled=True))


def total_over_devices(term_in, term_out):
    size = lax.axis_size("slab") * lax.axis_size("batch")
    axes = ("batch", "slab")
    both = jnp.concatenate([term_in.reshape(-1), term_out.reshape(-1)]).reshape(size, -1)
    shares = lax.all_to_all(both, axes, split_axis=0, concat_axis=0, tiled=True)
    total = lax.all_gather(jnp.sum(shares, axis=0), axes, axis=0, tiled=True)
    count = term_in.size
    return (total[:count].reshape(term_in.shape), total[count:].reshape(term_out.shape))


def shards(field, cotangent, spectral_weight, w_in, w_out):
    cells = NX * NY * NZ
    sample = field[0]
    upstream = cotangent[0]
    spectrum = gather_modes(forward_xy(sample)).astype(jnp.bfloat16)
    mixed_modes = mode_product(spectrum, spectral_weight)
    spatial = (return_slabs(inverse_z(mixed_modes, NZ)) / cells).astype(jnp.bfloat16)
    grad_field, term_in, term_out = mlp_planes(sample, spatial, upstream, w_in, w_out)
    in_total, out_total = total_over_devices(term_in, term_out)
    tokens = lax.axis_size("slab") * lax.axis_size("batch") * sample.shape[0] * NX * NY
    norm_scale = 1.0 / math.sqrt(tokens)
    grad_modes = (gather_modes(forward_xy(grad_field.astype(jnp.bfloat16))) / cells).astype(
        jnp.bfloat16
    )
    sample_term = lax.optimization_barrier(weight_term(spectrum, grad_modes).astype(jnp.bfloat16))
    summed = lax.psum_scatter(
        sample_term.astype(jnp.float32).astype(jnp.bfloat16),
        "batch",
        scatter_dimension=0,
        tiled=True,
    )
    back_modes = adjoint_product(spectral_weight, grad_modes)
    adjoint = return_slabs(inverse_z(back_modes, NZ))
    field_grad = (grad_field + adjoint).astype(jnp.bfloat16)
    return (field_grad[None], summed, in_total * norm_scale, out_total * norm_scale)


def solution(mesh):
    in_specs = (
        P("batch", "slab", None, None, None),
        P("batch", "slab", None, None, None),
        P(None, None, None, "slab"),
        P(),
        P(),
    )
    out_specs = (P("batch", "slab", None, None, None), P("batch", None, None, "slab"), P(), P())
    return jax.shard_map(shards, mesh=mesh, in_specs=in_specs, out_specs=out_specs, check_vma=False)
```

```python
import math

import jax
import jax.numpy as jnp
import numpy as np
from jax import lax
from jax.experimental import pallas as pl
from jax.experimental.pallas import tpu as pltpu
from jax.sharding import PartitionSpec as P

NX = 128
NY = 128
NZ = 128
KX = 32
KY = 32
KZ = 16


def product_of(pattern, first_op, second_op):
    return jnp.einsum(pattern, first_op, second_op, preferred_element_type=jnp.float32)


def tables(length, kept_modes):
    position = jnp.arange(length, dtype=jnp.int32)[:, None]
    frequency = jnp.arange(kept_modes, dtype=jnp.int32)[None, :]
    phases = (position * frequency % length).astype(jnp.float32)
    angles = phases * (2.0 * math.pi / length)
    return (jnp.cos(angles), jnp.sin(angles))


def forward_xy(field_part):
    depth_len, channels, x_len = (field_part.shape[0], field_part.shape[1], field_part.shape[2])
    cos_y, sin_y = tables(field_part.shape[3], KY)
    table_y = jnp.concatenate([cos_y, -sin_y], axis=1).astype(jnp.bfloat16)
    halfway = product_of("zcxy,yk->zckx", field_part, table_y).astype(jnp.bfloat16)
    stacked = halfway.reshape(depth_len, channels, 2, KY, x_len)
    cos_x, sin_x = tables(x_len, KX)
    table_x = jnp.stack([cos_x, sin_x]).astype(jnp.bfloat16)
    parts = product_of("zcpkx,qxj->pqzcjk", stacked, table_x)
    real_xy = parts[0, 0] + parts[1, 1]
    imag_xy = parts[1, 0] - parts[0, 1]
    return jnp.stack(
        [real_xy.reshape(depth_len, channels, -1), imag_xy.reshape(depth_len, channels, -1)]
    )


GROUP = 8


def depth_matrix(slabs):
    planes = NZ // slabs
    position = np.arange(NZ)[:, None] * np.arange(KZ)[None, :] % NZ
    angles = position * (2.0 * math.pi / NZ)
    cos_z, sin_z = np.cos(angles), np.sin(angles)
    blocks = np.stack([np.stack([cos_z, -sin_z], 1), np.stack([sin_z, cos_z], 1)], 1)
    blocks = blocks.reshape(slabs, planes, 2, 2, KZ)
    matrix = np.einsum("szpqk,mn->spzmqnk", blocks, np.eye(GROUP))
    return matrix.reshape(slabs * 2 * planes * GROUP, 2 * GROUP * KZ).astype(jnp.bfloat16)


def forward_z(received, channels):
    matrix = jnp.asarray(depth_matrix(lax.axis_size("slab")))
    out = lax.dot_general(
        received, matrix, (((0,), (0,)), ((), ())), preferred_element_type=jnp.float32
    )
    out = out.reshape(-1, channels, 2, GROUP * KZ)
    return jnp.transpose(out, (2, 1, 0, 3)).reshape(2, channels, -1)


def inverse_z(profile_modes):
    matrix = jnp.asarray(depth_matrix(lax.axis_size("slab")))
    return jnp.dot(matrix, profile_modes, preferred_element_type=jnp.float32).astype(jnp.bfloat16)


def inverse_xy(spectra):
    depth_len, channels = (spectra.shape[1], spectra.shape[2])
    stacked = spectra.reshape(2, depth_len, channels, KX, KY)
    cos_x, sin_x = tables(NX, KX)
    table_x = jnp.stack([cos_x, sin_x]).astype(jnp.bfloat16)
    parts = product_of("pzcjk,qxj->pqzckx", stacked, table_x)
    real_x = parts[0, 0] - parts[1, 1]
    imag_x = parts[0, 1] + parts[1, 0]
    rows = jnp.stack([real_x, imag_x]).astype(jnp.bfloat16)
    cos_y, sin_y = tables(NY, KY)
    table_y = jnp.stack([cos_y, -sin_y]).astype(jnp.bfloat16)
    return product_of("pzckx,pyk->zcxy", rows, table_y)


LANES = 128
PART = 8


def mode_kernel(s_ref, w_ref, o_ref):
    @pl.when(pl.program_id(0) == 0)
    def _():
        o_ref[...] = jnp.zeros_like(o_ref)

    for start in range(0, o_ref.shape[2], LANES):
        at = pl.ds(start, LANES)
        real, imag = o_ref[0, :, at], o_ref[1, :, at]
        for c in range(s_ref.shape[1]):
            s_real, s_imag = s_ref[0, c : c + 1, at], s_ref[1, c : c + 1, at]
            w_real = w_ref[0, c, :, at].astype(jnp.float32)
            w_imag = w_ref[1, c, :, at].astype(jnp.float32)
            real += s_real * w_real - s_imag * w_imag
            imag += s_real * w_imag + s_imag * w_real
        o_ref[0, :, at] = real
        o_ref[1, :, at] = imag


def mode_product(spectrum, weight):
    _, c_in, c_out, modes = weight.shape
    return pl.pallas_call(
        mode_kernel,
        grid=(c_in // PART,),
        in_specs=[
            pl.BlockSpec((2, PART, modes), lambda i: (0, i, 0)),
            pl.BlockSpec((2, PART, c_out, modes), lambda i: (0, i, 0, 0)),
        ],
        out_specs=pl.BlockSpec((2, c_out, modes), lambda i: (0, 0, 0)),
        out_shape=jax.ShapeDtypeStruct((2, c_out, modes), jnp.float32),
        compiler_params=pltpu.CompilerParams(vmem_limit_bytes=32 * 1024 * 1024),
    )(spectrum.astype(jnp.float32), weight)


def adjoint_kernel(s_ref, g_ref, w_ref, b_ref, t_ref):
    for start in range(0, g_ref.shape[2], LANES):
        at = pl.ds(start, LANES)
        g_real, g_imag = g_ref[0, :, at], g_ref[1, :, at]
        for c in range(s_ref.shape[1]):
            s_real, s_imag = s_ref[0, c : c + 1, at], s_ref[1, c : c + 1, at]
            t_ref[0, c, :, at] = (s_real * g_real + s_imag * g_imag).astype(t_ref.dtype)
            t_ref[1, c, :, at] = (s_real * g_imag - s_imag * g_real).astype(t_ref.dtype)
            w_real = w_ref[0, c, :, at].astype(jnp.float32)
            w_imag = w_ref[1, c, :, at].astype(jnp.float32)
            b_ref[0, c : c + 1, at] = jnp.sum(
                w_real * g_real + w_imag * g_imag, axis=0, keepdims=True
            )
            b_ref[1, c : c + 1, at] = jnp.sum(
                w_real * g_imag - w_imag * g_real, axis=0, keepdims=True
            )


def adjoint_and_term(spectrum, grad_modes, weight):
    _, c_in, c_out, modes = weight.shape
    small = pl.BlockSpec((2, PART, modes), lambda i: (0, i, 0))
    large = pl.BlockSpec((2, PART, c_out, modes), lambda i: (0, i, 0, 0))
    return pl.pallas_call(
        adjoint_kernel,
        grid=(c_in // PART,),
        in_specs=[small, pl.BlockSpec((2, c_out, modes), lambda i: (0, 0, 0)), large],
        out_specs=[small, large],
        out_shape=[
            jax.ShapeDtypeStruct((2, c_in, modes), jnp.float32),
            jax.ShapeDtypeStruct(weight.shape, jnp.bfloat16),
        ],
        compiler_params=pltpu.CompilerParams(vmem_limit_bytes=32 * 1024 * 1024),
    )(spectrum.astype(jnp.float32), grad_modes.astype(jnp.float32), weight)


def inner_last(first_op, second_op):
    return lax.dot_general(
        first_op, second_op, (((1,), (1,)), ((), ())), preferred_element_type=jnp.float32
    )


GELU_A = math.sqrt(2.0 / math.pi)
GELU_B = GELU_A * 0.044715
ROWS = 16
CHUNK = 512


def mlp_kernel(f_ref, s_ref, u_ref, wt_ref, wo_ref, wi_ref, g_ref, ti_ref, to_ref, m_buf, u_buf, g_buf):
    first = (pl.program_id(0) == 0) & (pl.program_id(1) == 0)

    @pl.when(first)
    def _():
        ti_ref[...] = jnp.zeros_like(ti_ref)
        to_ref[...] = jnp.zeros_like(to_ref)

    channels, cells = m_buf.shape
    mixed = f_ref[0].astype(jnp.float32) + s_ref[0].astype(jnp.float32)
    m_buf[...] = mixed.reshape(channels, cells).astype(jnp.bfloat16)
    u_buf[...] = u_ref[0].astype(jnp.float32).reshape(channels, cells).astype(jnp.bfloat16)

    def step(i, _):
        at = pl.ds(pl.multiple_of(i * CHUNK, CHUNK), CHUNK)
        m = m_buf[:, at]
        u = u_buf[:, at]
        x = jnp.dot(wt_ref[...], m, preferred_element_type=jnp.float32)
        back = jnp.dot(wo_ref[...], u, preferred_element_type=jnp.float32)
        sq = x * x
        t = jnp.tanh(x * (GELU_A + GELU_B * sq))
        half = 0.5 + 0.5 * t
        act = x * half
        slope = half + act * (1.0 - t) * (GELU_A + (3.0 * GELU_B) * sq)
        pre_grad = (slope * back).astype(jnp.bfloat16)
        act = act.astype(jnp.bfloat16)
        g = u.astype(jnp.float32) + jnp.dot(
            wi_ref[...], pre_grad, preferred_element_type=jnp.float32
        )
        g_buf[:, at] = g
        ti_ref[...] += inner_last(m, pre_grad)
        to_ref[...] += inner_last(act, u)
        return 0

    lax.fori_loop(0, cells // CHUNK, step, 0)
    g_ref[0] = g_buf[...].reshape(g_ref.shape[1:]).astype(g_ref.dtype)


def mlp_planes(field_part, spatial, upstream, w_in, w_out):
    depth, channels, x_len, y_len = field_part.shape
    hidden = w_in.shape[1]
    block = pl.BlockSpec((1, channels, ROWS, y_len), lambda z, i: (z, 0, i, 0))
    whole = lambda shape: pl.BlockSpec(shape, lambda z, i: (0, 0))
    cells = ROWS * y_len
    return pl.pallas_call(
        mlp_kernel,
        grid=(depth, x_len // ROWS),
        in_specs=[block, block, block, whole((hidden, channels)), whole((hidden, channels)), whole((channels, hidden))],
        out_specs=[block, whole((channels, hidden)), whole((hidden, channels))],
        out_shape=[
            jax.ShapeDtypeStruct(field_part.shape, jnp.bfloat16),
            jax.ShapeDtypeStruct((channels, hidden), jnp.float32),
            jax.ShapeDtypeStruct((hidden, channels), jnp.float32),
        ],
        scratch_shapes=[
            pltpu.VMEM((channels, cells), jnp.bfloat16),
            pltpu.VMEM((channels, cells), jnp.bfloat16),
            pltpu.VMEM((channels, cells), jnp.float32),
        ],
        compiler_params=pltpu.CompilerParams(vmem_limit_bytes=48 * 1024 * 1024),
    )(field_part, spatial, upstream, w_in.T, w_out, w_in)


def gather_modes(spectra):
    slabs = lax.axis_size("slab")
    planes, channels = (spectra.shape[1], spectra.shape[2])
    split = spectra.astype(jnp.bfloat16).reshape(2, planes, channels, slabs, -1, GROUP)
    outgoing = jnp.transpose(split, (3, 0, 1, 5, 4, 2)).reshape(slabs * 2 * planes * GROUP, -1)
    received = lax.all_to_all(outgoing, "slab", split_axis=0, concat_axis=0, tiled=True)
    return forward_z(received, channels)


def return_slabs(modes):
    slabs = lax.axis_size("slab")
    planes, channels = (NZ // slabs, modes.shape[1])
    split = modes.astype(jnp.bfloat16).reshape(2, channels, -1, GROUP * KZ)
    stacked = jnp.transpose(split, (0, 3, 2, 1)).reshape(2 * GROUP * KZ, -1)
    profiles = inverse_z(stacked)
    received = lax.all_to_all(profiles, "slab", split_axis=0, concat_axis=0, tiled=True)
    received = received.reshape(slabs, 2, planes, GROUP, -1, channels)
    spectra = jnp.transpose(received, (1, 2, 5, 0, 4, 3)).reshape(2, planes, channels, -1)
    return inverse_xy(spectra)


def total_over_devices(term_in, term_out):
    size = lax.axis_size("slab") * lax.axis_size("batch")
    axes = ("batch", "slab")
    both = jnp.concatenate([term_in.reshape(-1), term_out.reshape(-1)]).reshape(size, -1)
    shares = lax.all_to_all(both, axes, split_axis=0, concat_axis=0, tiled=True)
    mine = jnp.broadcast_to(jnp.sum(shares, axis=0, keepdims=True), both.shape)
    total = lax.all_to_all(mine, axes, split_axis=0, concat_axis=0, tiled=True).reshape(-1)
    count = term_in.size
    return (total[:count].reshape(term_in.shape), total[count:].reshape(term_out.shape))


def shards(field, cotangent, spectral_weight, w_in, w_out):
    cells = NX * NY * NZ
    sample = field[0]
    upstream = cotangent[0]
    spectrum = gather_modes(forward_xy(sample)).astype(jnp.bfloat16)
    mixed_modes = mode_product(spectrum, spectral_weight)
    spatial = (return_slabs(mixed_modes) / cells).astype(jnp.bfloat16)
    grad_field, term_in, term_out = mlp_planes(sample, spatial, upstream, w_in, w_out)
    in_total, out_total = total_over_devices(term_in, term_out)
    tokens = lax.axis_size("slab") * lax.axis_size("batch") * sample.shape[0] * NX * NY
    norm_scale = 1.0 / math.sqrt(tokens)
    grad_modes = (gather_modes(forward_xy(grad_field.astype(jnp.bfloat16))) / cells).astype(
        jnp.bfloat16
    )
    back_modes, sample_term = adjoint_and_term(spectrum, grad_modes, spectral_weight)
    summed = lax.psum_scatter(
        sample_term,
        "batch",
        scatter_dimension=0,
        tiled=True,
    )
    adjoint = return_slabs(back_modes)
    field_grad = (grad_field + adjoint).astype(jnp.bfloat16)
    return (field_grad[None], summed, in_total * norm_scale, out_total * norm_scale)


def solution(mesh):
    in_specs = (
        P("batch", "slab", None, None, None),
        P("batch", "slab", None, None, None),
        P(None, None, None, "slab"),
        P(),
        P(),
    )
    out_specs = (P("batch", "slab", None, None, None), P("batch", None, None, "slab"), P(), P())
    return jax.shard_map(shards, mesh=mesh, in_specs=in_specs, out_specs=out_specs, check_vma=False)
```

```python
import math

import jax
import jax.numpy as jnp
import numpy as np
from jax import lax
from jax.experimental import pallas as pl
from jax.experimental.pallas import tpu as pltpu
from jax.sharding import PartitionSpec as P

NX = 128
NY = 128
NZ = 128
KX = 32
KY = 32
KZ = 16


def product_of(pattern, first_op, second_op):
    return jnp.einsum(pattern, first_op, second_op, preferred_element_type=jnp.float32)


def tables(length, kept_modes):
    position = jnp.arange(length, dtype=jnp.int32)[:, None]
    frequency = jnp.arange(kept_modes, dtype=jnp.int32)[None, :]
    phases = (position * frequency % length).astype(jnp.float32)
    angles = phases * (2.0 * math.pi / length)
    return (jnp.cos(angles), jnp.sin(angles))


def forward_xy(field_part):
    depth_len, channels, x_len = (field_part.shape[0], field_part.shape[1], field_part.shape[2])
    cos_y, sin_y = tables(field_part.shape[3], KY)
    table_y = jnp.concatenate([cos_y, -sin_y], axis=1).astype(jnp.bfloat16)
    halfway = product_of("zcxy,yk->zckx", field_part, table_y).astype(jnp.bfloat16)
    stacked = halfway.reshape(depth_len, channels, 2, KY, x_len)
    cos_x, sin_x = tables(x_len, KX)
    table_x = jnp.stack([cos_x, sin_x]).astype(jnp.bfloat16)
    parts = product_of("zcpkx,qxj->pqzcjk", stacked, table_x)
    real_xy = parts[0, 0] + parts[1, 1]
    imag_xy = parts[1, 0] - parts[0, 1]
    return jnp.stack(
        [real_xy.reshape(depth_len, channels, -1), imag_xy.reshape(depth_len, channels, -1)]
    )


GROUP = 8


def depth_matrix(slabs):
    planes = NZ // slabs
    position = np.arange(NZ)[:, None] * np.arange(KZ)[None, :] % NZ
    angles = position * (2.0 * math.pi / NZ)
    cos_z, sin_z = np.cos(angles), np.sin(angles)
    blocks = np.stack([np.stack([cos_z, -sin_z], 1), np.stack([sin_z, cos_z], 1)], 1)
    blocks = blocks.reshape(slabs, planes, 2, 2, KZ)
    matrix = np.einsum("szpqk,mn->spzmqnk", blocks, np.eye(GROUP))
    return matrix.reshape(slabs * 2 * planes * GROUP, 2 * GROUP * KZ).astype(jnp.bfloat16)


def forward_z(received, channels):
    matrix = jnp.asarray(depth_matrix(lax.axis_size("slab")))
    out = lax.dot_general(
        received, matrix, (((0,), (0,)), ((), ())), preferred_element_type=jnp.float32
    )
    out = out.reshape(-1, channels, 2, GROUP * KZ)
    return jnp.transpose(out, (2, 1, 0, 3)).reshape(2, channels, -1)


def inverse_z(profile_modes):
    matrix = jnp.asarray(depth_matrix(lax.axis_size("slab")))
    return jnp.dot(matrix, profile_modes, preferred_element_type=jnp.float32).astype(jnp.bfloat16)


def inverse_xy(spectra):
    depth_len, channels = (spectra.shape[1], spectra.shape[2])
    stacked = spectra.reshape(2, depth_len, channels, KX, KY)
    cos_x, sin_x = tables(NX, KX)
    table_x = jnp.stack([cos_x, sin_x]).astype(jnp.bfloat16)
    parts = product_of("pzcjk,qxj->pqzckx", stacked, table_x)
    real_x = parts[0, 0] - parts[1, 1]
    imag_x = parts[0, 1] + parts[1, 0]
    rows = jnp.stack([real_x, imag_x]).astype(jnp.bfloat16)
    cos_y, sin_y = tables(NY, KY)
    table_y = jnp.stack([cos_y, -sin_y]).astype(jnp.bfloat16)
    return product_of("pzckx,pyk->zcxy", rows, table_y)


LANES = 128
PART = 8


def mode_kernel(s_ref, w_ref, o_ref):
    @pl.when(pl.program_id(0) == 0)
    def _():
        o_ref[...] = jnp.zeros_like(o_ref)

    for start in range(0, o_ref.shape[2], LANES):
        at = pl.ds(start, LANES)
        real, imag = o_ref[0, :, at], o_ref[1, :, at]
        for c in range(s_ref.shape[1]):
            s_real, s_imag = s_ref[0, c : c + 1, at], s_ref[1, c : c + 1, at]
            w_real = w_ref[0, c, :, at].astype(jnp.float32)
            w_imag = w_ref[1, c, :, at].astype(jnp.float32)
            real += s_real * w_real - s_imag * w_imag
            imag += s_real * w_imag + s_imag * w_real
        o_ref[0, :, at] = real
        o_ref[1, :, at] = imag


def mode_product(spectrum, weight):
    _, c_in, c_out, modes = weight.shape
    return pl.pallas_call(
        mode_kernel,
        grid=(c_in // PART,),
        in_specs=[
            pl.BlockSpec((2, PART, modes), lambda i: (0, i, 0)),
            pl.BlockSpec((2, PART, c_out, modes), lambda i: (0, i, 0, 0)),
        ],
        out_specs=pl.BlockSpec((2, c_out, modes), lambda i: (0, 0, 0)),
        out_shape=jax.ShapeDtypeStruct((2, c_out, modes), jnp.float32),
        compiler_params=pltpu.CompilerParams(vmem_limit_bytes=32 * 1024 * 1024),
    )(spectrum.astype(jnp.float32), weight)


def adjoint_kernel(s_ref, g_ref, w_ref, b_ref, t_ref):
    for start in range(0, g_ref.shape[2], LANES):
        at = pl.ds(start, LANES)
        g_real, g_imag = g_ref[0, :, at], g_ref[1, :, at]
        for c in range(s_ref.shape[1]):
            s_real, s_imag = s_ref[0, c : c + 1, at], s_ref[1, c : c + 1, at]
            t_ref[0, c, :, at] = (s_real * g_real + s_imag * g_imag).astype(t_ref.dtype)
            t_ref[1, c, :, at] = (s_real * g_imag - s_imag * g_real).astype(t_ref.dtype)
            w_real = w_ref[0, c, :, at].astype(jnp.float32)
            w_imag = w_ref[1, c, :, at].astype(jnp.float32)
            b_ref[0, c : c + 1, at] = jnp.sum(
                w_real * g_real + w_imag * g_imag, axis=0, keepdims=True
            )
            b_ref[1, c : c + 1, at] = jnp.sum(
                w_real * g_imag - w_imag * g_real, axis=0, keepdims=True
            )


def adjoint_and_term(spectrum, grad_modes, weight):
    _, c_in, c_out, modes = weight.shape
    small = pl.BlockSpec((2, PART, modes), lambda i: (0, i, 0))
    large = pl.BlockSpec((2, PART, c_out, modes), lambda i: (0, i, 0, 0))
    return pl.pallas_call(
        adjoint_kernel,
        grid=(c_in // PART,),
        in_specs=[small, pl.BlockSpec((2, c_out, modes), lambda i: (0, 0, 0)), large],
        out_specs=[small, large],
        out_shape=[
            jax.ShapeDtypeStruct((2, c_in, modes), jnp.float32),
            jax.ShapeDtypeStruct(weight.shape, jnp.bfloat16),
        ],
        compiler_params=pltpu.CompilerParams(vmem_limit_bytes=32 * 1024 * 1024),
    )(spectrum.astype(jnp.float32), grad_modes.astype(jnp.float32), weight)


def inner_last(first_op, second_op):
    return lax.dot_general(
        first_op, second_op, (((1,), (1,)), ((), ())), preferred_element_type=jnp.float32
    )


GELU_A = math.sqrt(2.0 / math.pi)
GELU_B = GELU_A * 0.044715
ROWS = 16
CHUNK = 2048


def mlp_kernel(f_ref, s_ref, u_ref, wt_ref, wo_ref, wi_ref, g_ref, ti_ref, to_ref, m_buf, u_buf, g_buf):
    first = (pl.program_id(0) == 0) & (pl.program_id(1) == 0)

    @pl.when(first)
    def _():
        ti_ref[...] = jnp.zeros_like(ti_ref)
        to_ref[...] = jnp.zeros_like(to_ref)

    channels, cells = m_buf.shape
    mixed = f_ref[0].astype(jnp.float32) + s_ref[0].astype(jnp.float32)
    m_buf[...] = mixed.reshape(channels, cells).astype(jnp.bfloat16)
    u_buf[...] = u_ref[0].astype(jnp.float32).reshape(channels, cells).astype(jnp.bfloat16)

    def step(i, _):
        at = pl.ds(pl.multiple_of(i * CHUNK, CHUNK), CHUNK)
        m = m_buf[:, at]
        u = u_buf[:, at]
        x = jnp.dot(wt_ref[...], m, preferred_element_type=jnp.float32).astype(jnp.bfloat16)
        back = jnp.dot(wo_ref[...], u, preferred_element_type=jnp.float32).astype(jnp.bfloat16)
        narrow = lambda value: jnp.asarray(value, jnp.bfloat16)
        sq = x * x
        t = jnp.tanh(x * (narrow(GELU_A) + narrow(GELU_B) * sq))
        half = narrow(0.5) + narrow(0.5) * t
        act = x * half
        slope = half + act * (narrow(1.0) - t) * (narrow(GELU_A) + narrow(3.0 * GELU_B) * sq)
        pre_grad = slope * back
        g = u.astype(jnp.float32) + jnp.dot(
            wi_ref[...], pre_grad, preferred_element_type=jnp.float32
        )
        g_buf[:, at] = g
        ti_ref[...] += inner_last(m, pre_grad)
        to_ref[...] += inner_last(act, u)
        return 0

    lax.fori_loop(0, cells // CHUNK, step, 0)
    g_ref[0] = g_buf[...].reshape(g_ref.shape[1:]).astype(g_ref.dtype)


def mlp_planes(field_part, spatial, upstream, w_in, w_out):
    depth, channels, x_len, y_len = field_part.shape
    hidden = w_in.shape[1]
    block = pl.BlockSpec((1, channels, ROWS, y_len), lambda z, i: (z, 0, i, 0))
    whole = lambda shape: pl.BlockSpec(shape, lambda z, i: (0, 0))
    cells = ROWS * y_len
    return pl.pallas_call(
        mlp_kernel,
        grid=(depth, x_len // ROWS),
        in_specs=[block, block, block, whole((hidden, channels)), whole((hidden, channels)), whole((channels, hidden))],
        out_specs=[block, whole((channels, hidden)), whole((hidden, channels))],
        out_shape=[
            jax.ShapeDtypeStruct(field_part.shape, jnp.bfloat16),
            jax.ShapeDtypeStruct((channels, hidden), jnp.float32),
            jax.ShapeDtypeStruct((hidden, channels), jnp.float32),
        ],
        scratch_shapes=[
            pltpu.VMEM((channels, cells), jnp.bfloat16),
            pltpu.VMEM((channels, cells), jnp.bfloat16),
            pltpu.VMEM((channels, cells), jnp.float32),
        ],
        compiler_params=pltpu.CompilerParams(vmem_limit_bytes=48 * 1024 * 1024),
    )(field_part, spatial, upstream, w_in.T, w_out, w_in)


def gather_modes(spectra):
    slabs = lax.axis_size("slab")
    planes, channels = (spectra.shape[1], spectra.shape[2])
    split = spectra.astype(jnp.bfloat16).reshape(2, planes, channels, slabs, -1, GROUP)
    outgoing = jnp.transpose(split, (3, 0, 1, 5, 4, 2)).reshape(slabs * 2 * planes * GROUP, -1)
    received = lax.all_to_all(outgoing, "slab", split_axis=0, concat_axis=0, tiled=True)
    return forward_z(received, channels)


def return_slabs(modes):
    slabs = lax.axis_size("slab")
    planes, channels = (NZ // slabs, modes.shape[1])
    split = modes.astype(jnp.bfloat16).reshape(2, channels, -1, GROUP * KZ)
    stacked = jnp.transpose(split, (0, 3, 2, 1)).reshape(2 * GROUP * KZ, -1)
    profiles = inverse_z(stacked)
    received = lax.all_to_all(profiles, "slab", split_axis=0, concat_axis=0, tiled=True)
    received = received.reshape(slabs, 2, planes, GROUP, -1, channels)
    spectra = jnp.transpose(received, (1, 2, 5, 0, 4, 3)).reshape(2, planes, channels, -1)
    return inverse_xy(spectra)


def total_over_devices(term_in, term_out):
    size = lax.axis_size("slab") * lax.axis_size("batch")
    axes = ("batch", "slab")
    both = jnp.concatenate([term_in.reshape(-1), term_out.reshape(-1)]).reshape(size, -1)
    shares = lax.all_to_all(both, axes, split_axis=0, concat_axis=0, tiled=True)
    mine = jnp.broadcast_to(jnp.sum(shares, axis=0, keepdims=True), both.shape)
    total = lax.all_to_all(mine, axes, split_axis=0, concat_axis=0, tiled=True).reshape(-1)
    count = term_in.size
    return (total[:count].reshape(term_in.shape), total[count:].reshape(term_out.shape))


def shards(field, cotangent, spectral_weight, w_in, w_out):
    cells = NX * NY * NZ
    sample = field[0]
    upstream = cotangent[0]
    spectrum = gather_modes(forward_xy(sample)).astype(jnp.bfloat16)
    mixed_modes = mode_product(spectrum, spectral_weight)
    spatial = (return_slabs(mixed_modes) / cells).astype(jnp.bfloat16)
    grad_field, term_in, term_out = mlp_planes(sample, spatial, upstream, w_in, w_out)
    in_total, out_total = total_over_devices(term_in, term_out)
    tokens = lax.axis_size("slab") * lax.axis_size("batch") * sample.shape[0] * NX * NY
    norm_scale = 1.0 / math.sqrt(tokens)
    grad_modes = (gather_modes(forward_xy(grad_field.astype(jnp.bfloat16))) / cells).astype(
        jnp.bfloat16
    )
    back_modes, sample_term = adjoint_and_term(spectrum, grad_modes, spectral_weight)
    summed = lax.psum_scatter(
        sample_term,
        "batch",
        scatter_dimension=0,
        tiled=True,
    )
    adjoint = return_slabs(back_modes)
    field_grad = (grad_field + adjoint).astype(jnp.bfloat16)
    return (field_grad[None], summed, in_total * norm_scale, out_total * norm_scale)


def solution(mesh):
    in_specs = (
        P("batch", "slab", None, None, None),
        P("batch", "slab", None, None, None),
        P(None, None, None, "slab"),
        P(),
        P(),
    )
    out_specs = (P("batch", "slab", None, None, None), P("batch", None, None, "slab"), P(), P())
    return jax.shard_map(shards, mesh=mesh, in_specs=in_specs, out_specs=out_specs, check_vma=False)
```
